32 devices in a mesh: sect: 2 (over core), cols: 16 (over z, y, x).
Axes of the slice: x: 2, y: 2, z: 4, core: 2. Of those that a mesh axis runs over, the one named last changes fastest.
Arguments:
- air_state: float32 [64, 6, 98304], P('sect', None, 'cols'), may hold values from -6 to 6
- mix_coef: float32 [64, 98304], P('sect', 'cols'), may hold values from 0.1 to 1600
- flux_scale: float32 [98304], P('cols'), may hold values from 0.5 to 4
- sea_state: float32 [6, 98304], P(None, ('sect', 'cols')), may hold values from -6 to 6
- sea_rate: float32 [98304], P(('sect', 'cols')), may hold values from 0.5 to 4
- block_counts: int32 [32, 48], P(('sect', 'cols')), may hold values from 1 to 256, 9830 in all within a row
- cell_column: int32 [393216], P(('sect', 'cols')), may hold values from 0 to 127
- cell_owner: int32 [393216, 1], P(('sect', 'cols')), may hold values from 0 to 31; in each aligned block of 12288 rows (0 to 12287, 12288 to 24575, ...) at most 480 rows name the same one
- cell_coef: float32 [393216], P(('sect', 'cols')), may hold values from 0.3 to 3
- cell_weight: float32 [393216], P(('sect', 'cols')), may hold values from 0.1 to 0.5
- slot_cell: int32 [491520], P(('sect', 'cols')), may hold values from 0 to 3071
- slot_frac: float32 [491520], P(('sect', 'cols')), may hold values from 0.2 to 1
Outputs:
- air_new: float32 [64, 6, 98304], P('sect', None, 'cols')
- sea_new: float32 [6, 98304], P(None, ('sect', 'cols'))
The draws below stay inside these ranges and needn't reach their ends.
Inputs may be any that keep to these rules, and one draw needn't show every extreme that they name: `cell_owner`: among the slots of one device (aligned blocks of 12288 rows) no surface device is named more than 480 times, and some surface device exactly 480 times. `block_counts`: each device's counts have the same sum, and one block of every device is full.
All inputs are finite; a program needn't handle non-finite values.
Results may differ from the reference program's by a relative error of at most 0.0003.
Values sent between devices are 32-bit elements; how exact they have to be, the bound alone decides.
A program may use at most 128 MiB of HBM per device.

```python
import math
import jax
import jax.numpy as jnp
import numpy as np
from jax import lax

TRACERS = 6
LEVELS = 64
BLOCK_COLS = 128
BLOCK_SLOTS = 256
SUBSTEPS = 2
COL_DEV = 6144
COLS = 98304
BLOCKS_DEV = 48
XC_DEV = 12288
XCELLS = 393216
CAP = 480
RECV = 15360
RSLOTS = 491520
SC_DEV = 3072
SURF = 98304
N_SECT = 2
N_COLS = 16


def draw_mix_coef(key, part):
    key_base = jax.random.fold_in(key, 11)
    key_pick = jax.random.fold_in(key, 12)
    key_strength = jax.random.fold_in(key, 13)
    key_forced = jax.random.fold_in(key, 14)
    base = jnp.exp(jax.random.uniform(key_base, (LEVELS, COLS), jnp.float32, math.log(0.1), math.log(4.0)))
    block_total = COLS // BLOCK_COLS
    chosen = jax.random.randint(key_pick, (block_total,), 0, 4) == 0
    forced = jnp.arange(block_total, dtype=jnp.int32) == jax.random.randint(key_forced, (), 0, block_total)
    chosen = jnp.logical_or(chosen, forced)
    strength = jnp.exp(jax.random.uniform(key_strength, (block_total,), jnp.float32, math.log(100.0), math.log(400.0)))
    factor = jnp.where(chosen, strength, jnp.float32(1.0))
    factor_cols = jnp.repeat(factor, BLOCK_COLS, total_repeat_length=COLS)
    level = jnp.arange(LEVELS, dtype=jnp.int32)[:, None]
    boosted = jnp.where(level < LEVELS - 1, base * factor_cols[None, :], base)
    return boosted.astype(jnp.float32)


def touch_ends(values, rng, least, high):
    longest = values.shape.index(max(values.shape))
    spots = []
    for shift in (0, 1):
        where = [jax.random.randint(jax.random.fold_in(rng, axis), (), 0, length) for axis, length in enumerate(values.shape)]
        where[longest] = (where[longest] + shift) % values.shape[longest]
        spots.append(tuple(where))
    return values.at[spots[0]].set(least).at[spots[1]].set(high)


def block_scale(rng, shape, shards, low, high):
    loudness, own = 1.0, jax.random.fold_in(rng, 6)
    for dim, blocks in shards:
        heights = jnp.exp(jax.random.uniform(jax.random.fold_in(own, dim), (blocks,), jnp.float32, low / len(shards), high / len(shards)))
        loudness = loudness * jnp.repeat(heights, shape[dim] // blocks).reshape([-1 if axis == dim else 1 for axis in range(len(shape))])
    return loudness


def length_profile(number_of, total, reach, lean):
    portions = [(1 << 20) // math.isqrt(rank ** lean) + 1 for rank in range(2, number_of + 1)]
    rest, counts = total - reach - (number_of - 1), [1] * (number_of - 1)
    while rest > 0:
        movable = [i for i in range(number_of - 1) if counts[i] < reach]
        pool, left = sum([portions[i] for i in movable]), rest
        for i in movable:
            extra = min(reach - counts[i], max(1, left * portions[i] // pool), rest)
            counts[i] = counts[i] + extra
            rest = rest - extra
    return np.array([reach] + counts)


def ragged(stream_key, amount, total, most, lean):
    if amount == 2:
        one = jax.random.randint(stream_key, (), max(1, total - most), min(most, total - 1) + 1)
        return jnp.stack([one, total - one])
    tallies = jnp.asarray(length_profile(amount, total, most, lean), jnp.int32)
    twos = (amount - 1) // 2
    giver, receiver = tallies[1:1 + 2 * twos:2], tallies[2:2 + 2 * twos:2]
    room = jnp.minimum(giver - 1, most - receiver)
    passed = jax.random.randint(jax.random.fold_in(stream_key, 1), (twos,), 0, 1 << 20) % (room + 1)
    tallies = tallies.at[1:1 + 2 * twos:2].set(giver - passed).at[2:2 + 2 * twos:2].set(receiver + passed)
    return tallies[jax.random.permutation(jax.random.fold_in(stream_key, 2), amount)]


def deal_out(stream_key, own, number, rows, count, top, bound, lean):
    sequence = jax.random.permutation(stream_key, count)
    crowded, ordinary = load_shares(count, rows * top, bound, lean, True), load_shares(count, rows * top, bound, lean, False)
    places = jnp.arange(count)

    def named(tallies, rotation):
        used = int((tallies > 0).sum())
        fixed = max(1, used // 4)
        moved = fixed + (places - fixed + rotation * (used - fixed)) % max(1, count - fixed)
        return jnp.zeros((count,), jnp.int32).at[sequence[jnp.where(places < fixed, places, moved)]].set(jnp.asarray(tallies, jnp.int32))

    tallies = jnp.where(number % 4 == 0, named(crowded, number // 4), named(ordinary, number - number // 4 - 1))
    mixed = jax.random.permutation(jax.random.fold_in(own, 3), count)
    giver, sink = mixed[0:count // 2 * 2:2], mixed[1:count // 2 * 2:2]
    slack = jnp.minimum(tallies[giver] - 1, bound - tallies[sink]) // 2
    slack = jnp.where((giver == sequence[0]) | (sink == sequence[0]) | (tallies[sink] == 0), 0, jnp.maximum(slack, 0))
    moved = jax.random.randint(jax.random.fold_in(own, 4), (count // 2,), 0, 1 << 20) % (slack + 1)
    tallies = tallies.at[giver].add(-moved).at[sink].add(moved)
    labels = jnp.searchsorted(jnp.cumsum(tallies), jnp.arange(rows * top), side="right").astype(jnp.int32)
    listing = labels.reshape(top, rows).T
    listing = listing[jax.random.permutation(jax.random.fold_in(own, 1), rows)]
    rotation = jax.random.randint(jax.random.fold_in(own, 2), (rows, 1), 0, top)
    return jnp.take_along_axis(listing, (jnp.arange(top)[None, :] + rotation) % top, axis=1)


def load_shares(amount, total, limit, skew, full):
    weights = [(1 << 20) // math.isqrt(standing ** skew) + 1 for standing in range(1, amount + 1)]
    largest = limit if full else min(limit, max(-(-total // amount), total * weights[0] // sum(weights)))
    least = 1 if total - largest >= amount - 1 else 0
    counts, surplus = [largest] + [least] * (amount - 1), total - largest - least * (amount - 1)
    while surplus > 0:
        movable = [i for i in range(1, amount) if counts[i] < largest] or [i for i in range(1, amount) if counts[i] < limit]
        pool, remaining = sum([weights[i] for i in movable]), surplus
        for i in movable:
            addition = min(limit - counts[i], max(1, remaining * weights[i] // pool), surplus)
            counts[i] = counts[i] + addition
            surplus = surplus - addition
    return np.array(counts)


def gaussian(key, extent, deviation, limit, shards=(), kind=jnp.bfloat16):
    loudness = block_scale(key, extent, shards, -0.22, 0.18) if shards else 1.0
    result = jax.random.normal(key, extent, jnp.float32) * deviation * loudness
    return jnp.minimum(jnp.maximum(result, -limit), limit).astype(kind)


def setup_inputs(seed: int = 0) -> dict:
    streams_of = jax.random.split(jax.random.key(seed), 13)
    air_state = gaussian(streams_of[0], (LEVELS, TRACERS, COLS), 1.0, 6.0, ((0, 2), (2, 16)), jnp.float32)
    mix_coef = draw_mix_coef(jax.random.fold_in(streams_of[12], 71), 0)
    flux_scale = jnp.clip(jnp.exp(math.log(4.0) - 2.0794415 * jax.random.uniform(streams_of[2], (COLS,), jnp.float32) ** block_scale(streams_of[2], (COLS,), ((0, 16),), -0.2, 0.2)), 0.5, 4.0)
    sea_state = gaussian(streams_of[3], (TRACERS, SURF), 1.0, 6.0, ((1, 32),), jnp.float32)
    sea_rate = jnp.clip(jnp.exp(math.log(4.0) - 2.0794415 * jax.random.uniform(streams_of[4], (SURF,), jnp.float32) ** block_scale(streams_of[4], (SURF,), ((0, 32),), -0.2, 0.2)), 0.5, 4.0)
    block_counts = jax.vmap(lambda own: ragged(own, BLOCKS_DEV, BLOCKS_DEV * BLOCK_SLOTS * 4 // 5, BLOCK_SLOTS, 2))(jax.random.split(streams_of[5], (N_SECT * N_COLS))).reshape((N_SECT * N_COLS, BLOCKS_DEV)).astype(jnp.int32)
    cell_column = touch_ends(jax.random.randint(streams_of[6], (XCELLS,), 0, BLOCK_COLS), jax.random.fold_in(streams_of[6], 1), 0, BLOCK_COLS - 1).astype(jnp.int32)
    cell_owner_keys = jax.random.split(jax.random.fold_in(streams_of[7], 1), XCELLS // XC_DEV)
    cell_owner_turns = jax.random.permutation(jax.random.fold_in(streams_of[7], 3), XCELLS // XC_DEV)
    cell_owner = jax.vmap(lambda own, number: deal_out(jax.random.fold_in(streams_of[7], 2), own, number, XC_DEV, N_SECT * N_COLS, 1, CAP, 2))(cell_owner_keys, cell_owner_turns).reshape((XCELLS, 1))
    cell_coef = jnp.clip(jnp.exp(math.log(3.0) - 2.3025851 * jax.random.uniform(streams_of[8], (XCELLS,), jnp.float32) ** block_scale(streams_of[8], (XCELLS,), ((0, 32),), -0.2, 0.2)), 0.3, 3.0)
    cell_weight = jnp.clip(jnp.exp(math.log(0.5) - 1.609438 * jax.random.uniform(streams_of[9], (XCELLS,), jnp.float32) ** block_scale(streams_of[9], (XCELLS,), ((0, 32),), -0.2, 0.2)), 0.1, 0.5)
    slot_cell = touch_ends(jax.random.randint(streams_of[10], (RSLOTS,), 0, SC_DEV), jax.random.fold_in(streams_of[10], 1), 0, SC_DEV - 1).astype(jnp.int32)
    slot_frac = jnp.clip(jnp.exp(math.log(1.0) - 1.609438 * jax.random.uniform(streams_of[11], (RSLOTS,), jnp.float32) ** block_scale(streams_of[11], (RSLOTS,), ((0, 32),), -0.2, 0.2)), 0.2, 1.0)
    return dict(air_state=air_state, mix_coef=mix_coef, flux_scale=flux_scale, sea_state=sea_state, sea_rate=sea_rate, block_counts=block_counts, cell_column=cell_column, cell_owner=cell_owner, cell_coef=cell_coef, cell_weight=cell_weight, slot_cell=slot_cell, slot_frac=slot_frac)


def reference(air_state, mix_coef, flux_scale, sea_state, sea_rate, block_counts, cell_column, cell_owner, cell_coef, cell_weight, slot_cell, slot_frac):
    devices = N_SECT * N_COLS

    def level_down(carried, inputs):
        under, upper_part = carried
        coupling, column_values = inputs
        denom = 1.0 + coupling + under
        part = (column_values + upper_part) / denom
        ratio = coupling / denom
        return (coupling * (1.0 - ratio), coupling * part), (part, denom)

    start = (jnp.zeros((COLS,), jnp.float32), jnp.zeros((TRACERS, COLS), jnp.float32))
    _, (parts, denoms) = lax.scan(level_down, start, (mix_coef, air_state))
    ratios = mix_coef / denoms
    resid = parts[-1]
    slope = flux_scale / denoms[-1]

    slots = jnp.arange(XCELLS, dtype=jnp.int32)
    device = slots // XC_DEV
    local = slots % XC_DEV
    block = local // BLOCK_SLOTS
    within = local % BLOCK_SLOTS
    live = (within < block_counts[device, block]).astype(jnp.float32)
    column = (device % N_COLS) * COL_DEV + block * BLOCK_COLS + cell_column
    owner = cell_owner[:, 0]

    def ranks_of(owners):
        onehot = (owners[:, None] == jnp.arange(devices, dtype=jnp.int32)[None, :]).astype(jnp.int32)
        return jnp.sum(jnp.cumsum(onehot, axis=0) * onehot, axis=1) - 1

    ranks = lax.map(ranks_of, owner.reshape(devices, XC_DEV)).reshape(XCELLS).astype(jnp.int32)
    arrive = owner * RECV + device * CAP + ranks
    surface_cell = owner * SC_DEV + slot_cell[arrive]
    fraction = slot_frac[arrive]
    gain = cell_coef * live
    coupling_cell = gain * fraction

    flux_col = jnp.zeros((TRACERS, COLS), jnp.float32)
    sea = sea_state
    for step in range(SUBSTEPS):
        bottom = resid + slope * flux_col
        at_cells = bottom[:, column]
        numer = jnp.zeros((TRACERS, SURF), jnp.float32).at[:, surface_cell].add(coupling_cell * at_cells)
        total = jnp.zeros((SURF,), jnp.float32).at[surface_cell].add(coupling_cell)
        sea = (sea + sea_rate * numer) / (1.0 + sea_rate * total)
        flux = cell_weight * gain * (sea[:, surface_cell] - at_cells)
        flux_col = jnp.zeros((TRACERS, COLS), jnp.float32).at[:, column].add(flux)
    bottom = resid + slope * flux_col

    def level_up(below, inputs):
        part, ratio = inputs
        value = part + ratio * below
        return value, value

    _, rising = lax.scan(level_up, bottom, (parts[:-1], ratios[:-1]), reverse=True)
    air_new = jnp.concatenate([rising, bottom[None]], axis=0)
    return air_new, sea
```

```python
import functools

import jax
import jax.numpy as jnp
from jax import lax
from jax.experimental import pallas as pl
from jax.experimental.pallas import tpu as pltpu
from jax.sharding import PartitionSpec as P

BLOCK_COLS = 128
BLOCK_SLOTS = 256
SUBSTEPS = 2
LANES = 128
COL_TILE = 1024
PARAMS = pltpu.CompilerParams(vmem_limit_bytes=40 * 1024 * 1024)


def split(value):
    high = value.astype(jnp.bfloat16).astype(jnp.float32)
    return high, value - high


def pair(ref, i):
    return jnp.concatenate([ref[pl.ds(2 * i, 1), :], ref[pl.ds(2 * i + 1, 1), :]], axis=1)


def wide(ref, i):
    return jnp.concatenate([ref[2 * i], ref[2 * i + 1]], axis=1)


def onehot(index, count):
    return lax.broadcasted_iota(jnp.int32, (count, index.shape[1]), 0) == index


def lanes_map(lane):
    return jnp.where(onehot(lane, LANES), 1.0, 0.0).astype(jnp.bfloat16)


def scatter_step(acc, values, row, lane, rows):
    mask = onehot(row, rows)
    high, low = split(values)
    left = [
        jnp.concatenate(
            [jnp.where(mask, part[q : q + 1], 0.0) for q in range(values.shape[0])], axis=0
        ).astype(jnp.bfloat16)
        for part in (high, low)
    ]
    lane_hot = lanes_map(lane)
    acc[...] += lax.dot_general(
        jnp.concatenate(left, axis=1),
        jnp.concatenate([lane_hot, lane_hot], axis=1),
        (((1,), (1,)), ((), ())),
        preferred_element_type=jnp.float32,
    )


def table_of(value):
    high, low = split(value)
    return jnp.concatenate([high, low], axis=1).astype(jnp.bfloat16)


def gather_step(table, row, lane, rows, count):
    lane_hot = lanes_map(lane)
    picked = jnp.dot(
        table, jnp.concatenate([lane_hot, lane_hot], axis=0), preferred_element_type=jnp.float32
    )
    mask = onehot(row, rows)
    return jnp.concatenate(
        [
            jnp.sum(jnp.where(mask, picked[q * rows : (q + 1) * rows], 0.0), axis=0, keepdims=True)
            for q in range(count)
        ],
        axis=0,
    )


def setup_kernel(devices, cap_rows, owner, column, coef, weight, counts, out, acc, offset):
    acc[...] = jnp.zeros_like(acc)
    offset[...] = jnp.zeros_like(offset)
    later = (
        lax.broadcasted_iota(jnp.int32, (BLOCK_SLOTS, BLOCK_SLOTS), 0)
        <= lax.broadcasted_iota(jnp.int32, (BLOCK_SLOTS, BLOCK_SLOTS), 1)
    )
    later = jnp.where(later, 1.0, 0.0).astype(jnp.bfloat16)
    within = lax.broadcasted_iota(jnp.int32, (1, BLOCK_SLOTS), 1)

    def block(i, _):
        own = pair(owner, i)
        named = jnp.where(onehot(own, devices), 1.0, 0.0)
        running = (
            jnp.dot(named.astype(jnp.bfloat16), later, preferred_element_type=jnp.float32)
            + offset[:, 0:1]
        )
        rank = (jnp.sum(named * running, axis=0, keepdims=True) - 1.0).astype(jnp.int32)
        offset[...] += jnp.broadcast_to(jnp.sum(named, axis=1, keepdims=True), offset.shape)
        live = within < counts[pl.ds(i, 1), 0:1]
        gain = jnp.where(live, pair(coef, i), 0.0)
        flow = pair(weight, i) * gain
        gain_high, gain_low = split(gain)
        flow_high, flow_low = split(flow)
        values = jnp.concatenate(
            [
                jnp.full((1, BLOCK_SLOTS), i, jnp.int32).astype(jnp.float32),
                pair(column, i).astype(jnp.float32),
                gain_high,
                gain_low,
                flow_high,
                flow_low,
            ],
            axis=0,
        )
        mask = onehot(own * cap_rows + rank // LANES, LANES)
        left = jnp.concatenate(
            [jnp.where(mask, values[q : q + 1], 0.0) for q in range(6)], axis=0
        ).astype(jnp.bfloat16)
        acc[...] += lax.dot_general(
            left,
            lanes_map(rank % LANES),
            (((1,), (1,)), ((), ())),
            preferred_element_type=jnp.float32,
        )
        return 0

    lax.fori_loop(0, owner.shape[0] // 2, block, 0)
    out[0] = acc[0:128]
    out[1] = acc[128:256]
    out[2] = acc[256:384] + acc[384:512]
    out[3] = acc[512:640] + acc[640:768]


def setup(owner, column, coef, weight, counts, devices, cap_rows):
    return pl.pallas_call(
        functools.partial(setup_kernel, devices, cap_rows),
        out_shape=jax.ShapeDtypeStruct((4, LANES, LANES), jnp.float32),
        scratch_shapes=[
            pltpu.VMEM((6 * LANES, LANES), jnp.float32),
            pltpu.VMEM((devices, LANES), jnp.float32),
        ],
        compiler_params=PARAMS,
    )(owner, column, coef, weight, counts)


def level_down(mix, air, k, under, carried):
    coupling = mix[k : k + 1, :]
    inverse = 1.0 / (1.0 + coupling + under)
    part = (air[k] + carried) * inverse
    ratio = coupling * inverse
    return part, ratio, inverse, ratio * (1.0 + under), coupling * part


def descend_end_kernel(air, mix, end):
    under = jnp.zeros((1, end.shape[1]), jnp.float32)
    carried = jnp.zeros((air.shape[1], end.shape[1]), jnp.float32)
    for k in range(air.shape[0]):
        _, _, _, under, carried = level_down(mix, air, k, under, carried)
    end[...] = jnp.concatenate([carried, under], axis=0)


def descend_end(air, mix):
    levels, tracers, columns = air.shape
    return pl.pallas_call(
        descend_end_kernel,
        grid=(columns // COL_TILE,),
        in_specs=[
            pl.BlockSpec((levels, tracers, COL_TILE), lambda j: (0, 0, j)),
            pl.BlockSpec((levels, COL_TILE), lambda j: (0, j)),
        ],
        out_specs=pl.BlockSpec((tracers + 1, COL_TILE), lambda j: (0, j)),
        out_shape=jax.ShapeDtypeStruct((tracers + 1, columns), jnp.float32),
        compiler_params=PARAMS,
    )(air, mix)


def descend_kernel(air, mix, start, last, parts, ratios, ends):
    levels, tracers, _ = air.shape
    carried = start[0:tracers, :]
    under = start[tracers : tracers + 1, :]
    for k in range(levels):
        part, ratio, inverse, under, carried = level_down(mix, air, k, under, carried)
        parts[k] = part
        if k == levels - 1:
            ratio = last[...] * inverse
        ratios[k : k + 1, :] = ratio
    value, factor = part, ratio
    ends[0, 0:tracers, :] = part
    ends[0, tracers : tracers + 1, :] = ratio
    for k in range(levels - 2, -1, -1):
        ratio = ratios[k : k + 1, :]
        value = parts[k] + ratio * value
        factor = ratio * factor
    ends[1, 0:tracers, :] = value
    ends[1, tracers : tracers + 1, :] = factor


def descend(air, mix, start, last):
    levels, tracers, columns = air.shape
    return pl.pallas_call(
        descend_kernel,
        grid=(columns // COL_TILE,),
        in_specs=[
            pl.BlockSpec((levels, tracers, COL_TILE), lambda j: (0, 0, j)),
            pl.BlockSpec((levels, COL_TILE), lambda j: (0, j)),
            pl.BlockSpec((tracers + 1, COL_TILE), lambda j: (0, j)),
            pl.BlockSpec((1, COL_TILE), lambda j: (0, j)),
        ],
        out_specs=[
            pl.BlockSpec((levels, tracers, COL_TILE), lambda j: (0, 0, j)),
            pl.BlockSpec((levels, COL_TILE), lambda j: (0, j)),
            pl.BlockSpec((2, tracers + 1, COL_TILE), lambda j: (0, 0, j)),
        ],
        out_shape=[
            jax.ShapeDtypeStruct(air.shape, jnp.float32),
            jax.ShapeDtypeStruct(mix.shape, jnp.float32),
            jax.ShapeDtypeStruct((2, tracers + 1, columns), jnp.float32),
        ],
        compiler_params=PARAMS,
    )(air, mix, start, last)


def ascend_kernel(parts, ratios, below, out):
    value = below[...]
    for k in range(parts.shape[0] - 1, -1, -1):
        value = parts[k] + ratios[k : k + 1, :] * value
        out[k] = value


def ascend(parts, ratios, below):
    levels, tracers, columns = parts.shape
    return pl.pallas_call(
        ascend_kernel,
        grid=(columns // COL_TILE,),
        in_specs=[
            pl.BlockSpec((levels, tracers, COL_TILE), lambda j: (0, 0, j)),
            pl.BlockSpec((levels, COL_TILE), lambda j: (0, j)),
            pl.BlockSpec((tracers, COL_TILE), lambda j: (0, j)),
        ],
        out_specs=pl.BlockSpec((levels, tracers, COL_TILE), lambda j: (0, 0, j)),
        out_shape=jax.ShapeDtypeStruct(parts.shape, jnp.float32),
        compiler_params=PARAMS,
    )(parts, ratios, below)


def send_kernel(tracers, resid, slope, flux, other, block, column, gain, out):
    rows = slope.shape[0]
    flux_col = flux[...] + other[...]
    bottom = resid[...] + jnp.concatenate([slope[...]] * tracers, axis=0) * flux_col
    table = table_of(bottom)

    def step(i, _):
        at = gather_step(table, pair(block, i), pair(column, i), rows, tracers)
        sent = jnp.concatenate(
            [at, pair(gain, i), jnp.zeros((7 - tracers, 2 * LANES), jnp.float32)], axis=0
        )
        out[2 * i] = sent[:, 0:LANES]
        out[2 * i + 1] = sent[:, LANES:]
        return 0

    lax.fori_loop(0, block.shape[0] // 2, step, 0, unroll=4)


def send(tracers, resid, slope, flux, other, block, column, gain):
    return pl.pallas_call(
        functools.partial(send_kernel, tracers),
        out_shape=jax.ShapeDtypeStruct((block.shape[0], 8, LANES), jnp.float32),
        compiler_params=PARAMS,
    )(resid, slope, flux, other, block, column, gain)


def surface_kernel(tracers, arrived, frac, row, lane, sea, rate, out, sea_new, acc):
    rows = rate.shape[0]
    acc[...] = jnp.zeros_like(acc)

    def gathering(i, _):
        came = wide(arrived, i)
        coupling = came[tracers : tracers + 1] * pair(frac, i)
        values = jnp.concatenate([came[0:tracers] * coupling, coupling], axis=0)
        scatter_step(acc, values, pair(row, i), pair(lane, i), rows)
        return 0

    lax.fori_loop(0, row.shape[0] // 2, gathering, 0, unroll=4)
    strength = rate[...]
    inverse = 1.0 / (1.0 + strength * acc[tracers * rows : (tracers + 1) * rows])
    for q in range(tracers):
        here = slice(q * rows, (q + 1) * rows)
        sea_new[here] = (sea[here] + strength * acc[here]) * inverse
    table = table_of(sea_new[...])

    def returning(i, _):
        seen = gather_step(table, pair(row, i), pair(lane, i), rows, tracers)
        sent = jnp.concatenate([seen, jnp.zeros((8 - tracers, 2 * LANES), jnp.float32)], axis=0)
        out[2 * i] = sent[:, 0:LANES]
        out[2 * i + 1] = sent[:, LANES:]
        return 0

    lax.fori_loop(0, row.shape[0] // 2, returning, 0, unroll=4)


def surface(tracers, arrived, frac, row, lane, sea, rate):
    return pl.pallas_call(
        functools.partial(surface_kernel, tracers),
        out_shape=[
            jax.ShapeDtypeStruct(arrived.shape, jnp.float32),
            jax.ShapeDtypeStruct(sea.shape, jnp.float32),
        ],
        scratch_shapes=[pltpu.VMEM(((tracers + 1) * rate.shape[0], LANES), jnp.float32)],
        compiler_params=PARAMS,
    )(arrived, frac, row, lane, sea, rate)


def collect_kernel(tracers, returned, sent, flow, block, column, flux):
    rows = flux.shape[0] // tracers
    flux[...] = jnp.zeros_like(flux)

    def step(i, _):
        values = (wide(returned, i) - wide(sent, i))[0:tracers] * pair(flow, i)
        scatter_step(flux, values, pair(block, i), pair(column, i), rows)
        return 0

    lax.fori_loop(0, block.shape[0] // 2, step, 0, unroll=4)


def collect(tracers, rows, returned, sent, flow, block, column):
    return pl.pallas_call(
        functools.partial(collect_kernel, tracers),
        out_shape=jax.ShapeDtypeStruct((tracers * rows, LANES), jnp.float32),
        compiler_params=PARAMS,
    )(returned, sent, flow, block, column)


def body(
    air_state,
    mix_coef,
    flux_scale,
    sea_state,
    sea_rate,
    block_counts,
    cell_column,
    cell_owner,
    cell_coef,
    cell_weight,
    slot_cell,
    slot_frac,
):
    levels, tracers, columns = air_state.shape
    is_lower = lax.axis_index("sect") == 1
    devices = lax.axis_size("sect") * lax.axis_size("cols")
    rows = columns // BLOCK_COLS
    surf_cells = sea_state.shape[1]
    surf_rows = surf_cells // LANES
    capacity = slot_cell.shape[0] // devices
    cap_rows = -(-capacity // LANES)
    padding = ((0, 0), (0, cap_rows * LANES - capacity))

    handed = lax.ppermute(descend_end(air_state, mix_coef), "sect", [(0, 1)])
    slots = setup(
        cell_owner.reshape(-1, LANES),
        cell_column.reshape(-1, LANES),
        cell_coef.reshape(-1, LANES),
        cell_weight.reshape(-1, LANES),
        jnp.broadcast_to(block_counts.reshape(-1, 1), (rows, LANES)),
        devices,
        cap_rows,
    )
    block = slots[0].astype(jnp.int32)
    column = slots[1].astype(jnp.int32)
    gain, flow = slots[2], slots[3]
    cell = jnp.pad(slot_cell.reshape(devices, capacity), padding).reshape(-1, LANES)
    frac = jnp.pad(slot_frac.reshape(devices, capacity), padding).reshape(-1, LANES)
    row, lane = cell // LANES, cell % LANES

    last = jnp.where(is_lower, flux_scale, mix_coef[-1])[None]
    parts, ratios, ends = descend(air_state, mix_coef, handed, last)
    received = lax.ppermute(ends, "sect", [(1, 0)])
    low = jnp.where(is_lower, ends, received)
    resid = low[0, :tracers].reshape(tracers * rows, LANES)
    slope = low[0, tracers].reshape(rows, LANES)

    sea = sea_state.reshape(tracers * surf_rows, LANES)
    rate = sea_rate.reshape(surf_rows, LANES)
    flux = other = jnp.zeros((tracers * rows, LANES), jnp.float32)
    for _ in range(SUBSTEPS):
        sent = send(tracers, resid, slope, flux, other, block, column, gain)
        arrived = lax.all_to_all(sent, ("sect", "cols"), split_axis=0, concat_axis=0, tiled=True)
        back, sea = surface(tracers, arrived, frac, row, lane, sea, rate)
        returned = lax.all_to_all(back, ("sect", "cols"), split_axis=0, concat_axis=0, tiled=True)
        flux = collect(tracers, rows, returned, sent, flow, block, column)
        other = lax.ppermute(flux, "sect", [(0, 1), (1, 0)])
    flux_col = (flux + other).reshape(tracers, columns)
    below = jnp.where(is_lower, flux_col, low[1, :tracers] + low[1, tracers] * flux_col)
    return (ascend(parts, ratios, below), sea.reshape(tracers, surf_cells))


def solution(mesh):
    return jax.shard_map(
        body,
        mesh=mesh,
        in_specs=(
            P("sect", None, "cols"),
            P("sect", "cols"),
            P("cols"),
            P(None, ("sect", "cols")),
            P(("sect", "cols")),
            P(("sect", "cols"), None),
            P(("sect", "cols")),
            P(("sect", "cols"), None),
            P(("sect", "cols")),
            P(("sect", "cols")),
            P(("sect", "cols")),
            P(("sect", "cols")),
        ),
        out_specs=(P("sect", None, "cols"), P(None, ("sect", "cols"))),
        check_vma=False,
    )
```

```python
import functools

import jax
import jax.numpy as jnp
from jax import lax
from jax.experimental import pallas as pl
from jax.experimental.pallas import tpu as pltpu
from jax.sharding import PartitionSpec as P

BLOCK_COLS = 128
BLOCK_SLOTS = 256
SUBSTEPS = 2
LANES = 128
COL_TILE = 1024
PARAMS = pltpu.CompilerParams(vmem_limit_bytes=40 * 1024 * 1024)


def split(value):
    high = value.astype(jnp.bfloat16).astype(jnp.float32)
    return high, value - high


def pair(ref, i):
    return jnp.concatenate([ref[pl.ds(2 * i, 1), :], ref[pl.ds(2 * i + 1, 1), :]], axis=1)


def onehot(index, count):
    return lax.broadcasted_iota(jnp.int32, (count, index.shape[1]), 0) == index


def lanes_map(lane):
    return jnp.where(onehot(lane, LANES), 1.0, 0.0).astype(jnp.bfloat16)


def scatter_step(acc, values, row, lane, rows):
    mask = onehot(row, rows)
    high, low = split(values)
    left = [
        jnp.concatenate(
            [jnp.where(mask, part[q : q + 1], 0.0) for q in range(values.shape[0])], axis=0
        ).astype(jnp.bfloat16)
        for part in (high, low)
    ]
    lane_hot = lanes_map(lane)
    acc[...] += lax.dot_general(
        jnp.concatenate(left, axis=1),
        jnp.concatenate([lane_hot, lane_hot], axis=1),
        (((1,), (1,)), ((), ())),
        preferred_element_type=jnp.float32,
    )


def table_of(value):
    high, low = split(value)
    return jnp.concatenate([high, low], axis=1).astype(jnp.bfloat16)


def gather_step(table, row, lane, rows, count):
    lane_hot = lanes_map(lane)
    picked = jnp.dot(
        table, jnp.concatenate([lane_hot, lane_hot], axis=0), preferred_element_type=jnp.float32
    )
    mask = onehot(row, rows)
    return jnp.concatenate(
        [
            jnp.sum(jnp.where(mask, picked[q * rows : (q + 1) * rows], 0.0), axis=0, keepdims=True)
            for q in range(count)
        ],
        axis=0,
    )


def setup_kernel(devices, cap_rows, owner, column, coef, weight, counts, out, acc, offset):
    acc[...] = jnp.zeros_like(acc)
    offset[...] = jnp.zeros_like(offset)
    later = (
        lax.broadcasted_iota(jnp.int32, (BLOCK_SLOTS, BLOCK_SLOTS), 0)
        <= lax.broadcasted_iota(jnp.int32, (BLOCK_SLOTS, BLOCK_SLOTS), 1)
    )
    later = jnp.where(later, 1.0, 0.0).astype(jnp.bfloat16)
    within = lax.broadcasted_iota(jnp.int32, (1, BLOCK_SLOTS), 1)

    def block(i, _):
        own = pair(owner, i)
        named = jnp.where(onehot(own, devices), 1.0, 0.0)
        running = (
            jnp.dot(named.astype(jnp.bfloat16), later, preferred_element_type=jnp.float32)
            + offset[:, 0:1]
        )
        rank = (jnp.sum(named * running, axis=0, keepdims=True) - 1.0).astype(jnp.int32)
        offset[...] += jnp.broadcast_to(jnp.sum(named, axis=1, keepdims=True), offset.shape)
        live = within < counts[pl.ds(i, 1), 0:1]
        gain = jnp.where(live, pair(coef, i), 0.0)
        flow = pair(weight, i) * gain
        gain_high, gain_low = split(gain)
        flow_high, flow_low = split(flow)
        values = jnp.concatenate(
            [
                jnp.full((1, BLOCK_SLOTS), i, jnp.int32).astype(jnp.float32),
                pair(column, i).astype(jnp.float32),
                gain_high,
                gain_low,
                flow_high,
                flow_low,
            ],
            axis=0,
        )
        mask = onehot(own * cap_rows + rank // LANES, LANES)
        left = jnp.concatenate(
            [jnp.where(mask, values[q : q + 1], 0.0) for q in range(6)], axis=0
        ).astype(jnp.bfloat16)
        acc[...] += lax.dot_general(
            left,
            lanes_map(rank % LANES),
            (((1,), (1,)), ((), ())),
            preferred_element_type=jnp.float32,
        )
        return 0

    lax.fori_loop(0, owner.shape[0] // 2, block, 0, unroll=4)
    out[0] = acc[0:128]
    out[1] = acc[128:256]
    out[2] = acc[256:384] + acc[384:512]
    out[3] = acc[512:640] + acc[640:768]


def setup(owner, column, coef, weight, counts, devices, cap_rows):
    return pl.pallas_call(
        functools.partial(setup_kernel, devices, cap_rows),
        out_shape=jax.ShapeDtypeStruct((4, LANES, LANES), jnp.float32),
        scratch_shapes=[
            pltpu.VMEM((6 * LANES, LANES), jnp.float32),
            pltpu.VMEM((devices, LANES), jnp.float32),
        ],
        compiler_params=PARAMS,
    )(owner, column, coef, weight, counts)


def level_down(mix, air, k, under, carried):
    coupling = mix[k : k + 1, :]
    inverse = 1.0 / (1.0 + coupling + under)
    part = (air[k] + carried) * inverse
    ratio = coupling * inverse
    return part, ratio, inverse, ratio * (1.0 + under), coupling * part


def descend_end_kernel(air, mix, end):
    under = jnp.zeros((1, end.shape[1]), jnp.float32)
    carried = jnp.zeros((air.shape[1], end.shape[1]), jnp.float32)
    for k in range(air.shape[0]):
        _, _, _, under, carried = level_down(mix, air, k, under, carried)
    end[...] = jnp.concatenate([carried, under], axis=0)


def descend_end(air, mix):
    levels, tracers, columns = air.shape
    return pl.pallas_call(
        descend_end_kernel,
        grid=(columns // COL_TILE,),
        in_specs=[
            pl.BlockSpec((levels, tracers, COL_TILE), lambda j: (0, 0, j)),
            pl.BlockSpec((levels, COL_TILE), lambda j: (0, j)),
        ],
        out_specs=pl.BlockSpec((tracers + 1, COL_TILE), lambda j: (0, j)),
        out_shape=jax.ShapeDtypeStruct((tracers + 1, columns), jnp.float32),
        compiler_params=PARAMS,
    )(air, mix)


def descend_kernel(air, mix, start, last, parts, ratios, ends):
    levels, tracers, _ = air.shape
    carried = start[0:tracers, :]
    under = start[tracers : tracers + 1, :]
    for k in range(levels):
        part, ratio, inverse, under, carried = level_down(mix, air, k, under, carried)
        parts[k] = part
        if k == levels - 1:
            ratio = last[...] * inverse
        ratios[k : k + 1, :] = ratio
    value, factor = part, ratio
    ends[0, 0:tracers, :] = part
    ends[0, tracers : tracers + 1, :] = ratio
    for k in range(levels - 2, -1, -1):
        ratio = ratios[k : k + 1, :]
        value = parts[k] + ratio * value
        factor = ratio * factor
    ends[1, 0:tracers, :] = value
    ends[1, tracers : tracers + 1, :] = factor


def descend(air, mix, start, last):
    levels, tracers, columns = air.shape
    return pl.pallas_call(
        descend_kernel,
        grid=(columns // COL_TILE,),
        in_specs=[
            pl.BlockSpec((levels, tracers, COL_TILE), lambda j: (0, 0, j)),
            pl.BlockSpec((levels, COL_TILE), lambda j: (0, j)),
            pl.BlockSpec((tracers + 1, COL_TILE), lambda j: (0, j)),
            pl.BlockSpec((1, COL_TILE), lambda j: (0, j)),
        ],
        out_specs=[
            pl.BlockSpec((levels, tracers, COL_TILE), lambda j: (0, 0, j)),
            pl.BlockSpec((levels, COL_TILE), lambda j: (0, j)),
            pl.BlockSpec((2, tracers + 1, COL_TILE), lambda j: (0, 0, j)),
        ],
        out_shape=[
            jax.ShapeDtypeStruct(air.shape, jnp.float32),
            jax.ShapeDtypeStruct(mix.shape, jnp.float32),
            jax.ShapeDtypeStruct((2, tracers + 1, columns), jnp.float32),
        ],
        compiler_params=PARAMS,
    )(air, mix, start, last)


def ascend_kernel(parts, ratios, below, out):
    value = below[...]
    for k in range(parts.shape[0] - 1, -1, -1):
        value = parts[k] + ratios[k : k + 1, :] * value
        out[k] = value


def ascend(parts, ratios, below):
    levels, tracers, columns = parts.shape
    return pl.pallas_call(
        ascend_kernel,
        grid=(columns // COL_TILE,),
        in_specs=[
            pl.BlockSpec((levels, tracers, COL_TILE), lambda j: (0, 0, j)),
            pl.BlockSpec((levels, COL_TILE), lambda j: (0, j)),
            pl.BlockSpec((tracers, COL_TILE), lambda j: (0, j)),
        ],
        out_specs=pl.BlockSpec((levels, tracers, COL_TILE), lambda j: (0, 0, j)),
        out_shape=jax.ShapeDtypeStruct(parts.shape, jnp.float32),
        compiler_params=PARAMS,
    )(parts, ratios, below)


def exchange_kernel(
    tracers,
    sections,
    ring,
    resid,
    slope,
    flux,
    other,
    block,
    column,
    flow,
    coupling,
    row,
    lane,
    sea,
    rate,
    flux_new,
    sea_new,
    sent,
    arrived,
    back,
    returned,
    acc,
    out_send,
    out_recv,
    back_send,
    back_recv,
):
    devices = sections * ring
    rows, surf_rows = slope.shape[0], rate.shape[0]
    parts = sent.shape[1] // tracers
    me = lax.axis_index("sect") * ring + lax.axis_index("cols")

    def coords(device):
        return (device // ring, lax.rem(device, ring))

    def ahead(s):
        return lax.rem(me + s, devices)

    def behind(s):
        return lax.rem(me + devices - s, devices)

    def outward(s):
        device = ahead(s)
        return pltpu.make_async_remote_copy(
            src_ref=sent.at[device],
            dst_ref=arrived.at[me],
            send_sem=out_send.at[s],
            recv_sem=out_recv.at[s],
            device_id=coords(device),
            device_id_type=pl.DeviceIdType.MESH,
        )

    def homeward(s):
        device = ahead(s)
        return pltpu.make_async_remote_copy(
            src_ref=back.at[device],
            dst_ref=returned.at[me],
            send_sem=back_send.at[s],
            recv_sem=back_recv.at[s],
            device_id=coords(device),
            device_id_type=pl.DeviceIdType.MESH,
        )

    def pack(values):
        return jnp.concatenate(
            [values[:, p * LANES : (p + 1) * LANES] for p in range(parts)], axis=0
        )

    def unpack(values):
        return jnp.concatenate(
            [values[p * tracers : (p + 1) * tracers] for p in range(parts)], axis=1
        )

    barrier = pltpu.get_barrier_semaphore()

    def greet(s, _):
        pl.semaphore_signal(
            barrier,
            inc=1,
            device_id=coords(ahead(s)),
            device_id_type=pl.DeviceIdType.MESH,
        )
        return 0

    lax.fori_loop(1, devices, greet, 0)
    bottom = resid[...] + jnp.concatenate([slope[...]] * tracers, axis=0) * (flux[...] + other[...])
    table = table_of(bottom)

    def at_cells(device):
        here = pl.ds(device, 1)
        return pack(gather_step(table, block[here, :], column[here, :], rows, tracers))

    own = at_cells(me)
    sent[me] = own
    pl.semaphore_wait(barrier, devices - 1)

    def send(s, _):
        device = ahead(s)
        sent[device] = at_cells(device)
        outward(s).start()
        return 0

    lax.fori_loop(1, devices, send, 0)
    acc[...] = jnp.zeros_like(acc)

    def add(values, device):
        here = pl.ds(device, 1)
        strength = coupling[here, :]
        scatter_step(
            acc,
            jnp.concatenate([unpack(values) * strength, strength], axis=0),
            row[here, :],
            lane[here, :],
            surf_rows,
        )

    add(own, me)

    def receive(s, _):
        outward(s).wait_recv()
        device = behind(s)
        add(arrived[device], device)
        return 0

    lax.fori_loop(1, devices, receive, 0)
    pace = rate[...]
    inverse = 1.0 / (1.0 + pace * acc[tracers * surf_rows : (tracers + 1) * surf_rows])
    for q in range(tracers):
        here = slice(q * surf_rows, (q + 1) * surf_rows)
        sea_new[here] = (sea[here] + pace * acc[here]) * inverse
    sea_table = table_of(sea_new[...])

    def seen(device):
        here = pl.ds(device, 1)
        return pack(gather_step(sea_table, row[here, :], lane[here, :], surf_rows, tracers))

    def give_back(s, _):
        device = ahead(s)
        back[device] = seen(device)
        homeward(s).start()
        return 0

    lax.fori_loop(1, devices, give_back, 0)
    flux_new[...] = jnp.zeros_like(flux_new)

    def collect(values, device):
        here = pl.ds(device, 1)
        scatter_step(
            flux_new,
            unpack(values - sent[device]) * flow[here, :],
            block[here, :],
            column[here, :],
            rows,
        )

    collect(seen(me), me)

    def take_back(s, _):
        homeward(s).wait_recv()
        device = behind(s)
        collect(returned[device], device)
        return 0

    lax.fori_loop(1, devices, take_back, 0)

    def finish(s, _):
        outward(s).wait_send()
        homeward(s).wait_send()
        return 0

    lax.fori_loop(1, devices, finish, 0)


def exchange(tracers, sections, ring, resid, slope, flux, other, block, column, flow, *surface):
    devices, slots = block.shape
    surf_rows = surface[-1].shape[0]
    landing = pltpu.VMEM((devices, tracers * slots // LANES, LANES), jnp.float32)
    return pl.pallas_call(
        functools.partial(exchange_kernel, tracers, sections, ring),
        out_shape=[
            jax.ShapeDtypeStruct(resid.shape, jnp.float32),
            jax.ShapeDtypeStruct((tracers * surf_rows, LANES), jnp.float32),
        ],
        in_specs=[pl.BlockSpec(memory_space=pltpu.VMEM)] * 12,
        out_specs=[pl.BlockSpec(memory_space=pltpu.VMEM)] * 2,
        scratch_shapes=[
            landing,
            landing,
            landing,
            landing,
            pltpu.VMEM(((tracers + 1) * surf_rows, LANES), jnp.float32),
            pltpu.SemaphoreType.DMA((devices,)),
            pltpu.SemaphoreType.DMA((devices,)),
            pltpu.SemaphoreType.DMA((devices,)),
            pltpu.SemaphoreType.DMA((devices,)),
        ],
        compiler_params=pltpu.CompilerParams(
            vmem_limit_bytes=40 * 1024 * 1024, collective_id=0, has_side_effects=True
        ),
    )(resid, slope, flux, other, block, column, flow, *surface)


def body(
    air_state,
    mix_coef,
    flux_scale,
    sea_state,
    sea_rate,
    block_counts,
    cell_column,
    cell_owner,
    cell_coef,
    cell_weight,
    slot_cell,
    slot_frac,
):
    levels, tracers, columns = air_state.shape
    is_lower = lax.axis_index("sect") == 1
    devices = lax.axis_size("sect") * lax.axis_size("cols")
    rows = columns // BLOCK_COLS
    surf_cells = sea_state.shape[1]
    surf_rows = surf_cells // LANES
    capacity = slot_cell.shape[0] // devices
    cap_rows = -(-capacity // LANES)
    padding = ((0, 0), (0, cap_rows * LANES - capacity))

    handed = lax.ppermute(descend_end(air_state, mix_coef), "sect", [(0, 1)])
    slots = setup(
        cell_owner.reshape(-1, LANES),
        cell_column.reshape(-1, LANES),
        cell_coef.reshape(-1, LANES),
        cell_weight.reshape(-1, LANES),
        jnp.broadcast_to(block_counts.reshape(-1, 1), (rows, LANES)),
        devices,
        cap_rows,
    )
    slots = slots.reshape(4, LANES * LANES)[:, : devices * cap_rows * LANES]
    slots = slots.reshape(4, devices, cap_rows * LANES)
    block = slots[0].astype(jnp.int32)
    column = slots[1].astype(jnp.int32)
    gain = lax.all_to_all(slots[2], ("sect", "cols"), split_axis=0, concat_axis=0, tiled=True)
    cell = jnp.pad(slot_cell.reshape(devices, capacity), padding)
    coupling = gain * jnp.pad(slot_frac.reshape(devices, capacity), padding)
    row, lane = cell // LANES, cell % LANES

    last = jnp.where(is_lower, flux_scale, mix_coef[-1])[None]
    parts, ratios, ends = descend(air_state, mix_coef, handed, last)
    received = lax.ppermute(ends, "sect", [(1, 0)])
    low = jnp.where(is_lower, ends, received)
    resid = low[0, :tracers].reshape(tracers * rows, LANES)
    slope = low[0, tracers].reshape(rows, LANES)

    sea = sea_state.reshape(tracers * surf_rows, LANES)
    rate = sea_rate.reshape(surf_rows, LANES)
    flux = other = jnp.zeros((tracers * rows, LANES), jnp.float32)
    for _ in range(SUBSTEPS):
        flux, sea = exchange(
            tracers,
            lax.axis_size("sect"),
            lax.axis_size("cols"),
            resid,
            slope,
            flux,
            other,
            block,
            column,
            slots[3],
            coupling,
            row,
            lane,
            sea,
            rate,
        )
        other = lax.ppermute(flux, "sect", [(0, 1), (1, 0)])
    flux_col = (flux + other).reshape(tracers, columns)
    below = jnp.where(is_lower, flux_col, low[1, :tracers] + low[1, tracers] * flux_col)
    return (ascend(parts, ratios, below), sea.reshape(tracers, surf_cells))


def solution(mesh):
    return jax.shard_map(
        body,
        mesh=mesh,
        in_specs=(
            P("sect", None, "cols"),
            P("sect", "cols"),
            P("cols"),
            P(None, ("sect", "cols")),
            P(("sect", "cols")),
            P(("sect", "cols"), None),
            P(("sect", "cols")),
            P(("sect", "cols"), None),
            P(("sect", "cols")),
            P(("sect", "cols")),
            P(("sect", "cols")),
            P(("sect", "cols")),
        ),
        out_specs=(P("sect", None, "cols"), P(None, ("sect", "cols"))),
        check_vma=False,
    )
```

```python
import functools

import jax
import jax.numpy as jnp
from jax import lax
from jax.experimental import pallas as pl
from jax.experimental.pallas import tpu as pltpu
from jax.sharding import PartitionSpec as P

BLOCK_COLS = 128
BLOCK_SLOTS = 256
SUBSTEPS = 2
LANES = 128
COL_TILE = 1024
PARAMS = pltpu.CompilerParams(vmem_limit_bytes=40 * 1024 * 1024)


def split(value):
    high = value.astype(jnp.bfloat16).astype(jnp.float32)
    return high, value - high


def pair(ref, i):
    return jnp.concatenate([ref[pl.ds(2 * i, 1), :], ref[pl.ds(2 * i + 1, 1), :]], axis=1)


def onehot(index, count):
    return lax.broadcasted_iota(jnp.int32, (count, index.shape[1]), 0) == index


def lanes_map(lane):
    return jnp.where(onehot(lane, LANES), 1.0, 0.0).astype(jnp.bfloat16)


def spread(mask, values):
    values = values.astype(jnp.bfloat16)
    return jnp.concatenate([mask * values[q : q + 1] for q in range(values.shape[0])], axis=0)


def one_hot(index, count):
    return jnp.where(onehot(index, count), 1.0, 0.0).astype(jnp.bfloat16)


def scatter_step(acc, values, row, lane, rows):
    mask = one_hot(row, rows)
    high, low = split(values)
    lane_hot = lanes_map(lane)
    acc[...] += lax.dot_general(
        jnp.concatenate([spread(mask, high), spread(mask, low)], axis=1),
        jnp.concatenate([lane_hot, lane_hot], axis=1),
        (((1,), (1,)), ((), ())),
        preferred_element_type=jnp.float32,
    )


def table_of(value):
    high, low = split(value)
    return jnp.concatenate([high, low], axis=1).astype(jnp.bfloat16)


def gather_step(table, row, lane, rows, count):
    lane_hot = lanes_map(lane)
    picked = jnp.dot(
        table, jnp.concatenate([lane_hot, lane_hot], axis=0), preferred_element_type=jnp.float32
    )
    mask = onehot(row, rows)
    return jnp.concatenate(
        [
            jnp.sum(jnp.where(mask, picked[q * rows : (q + 1) * rows], 0.0), axis=0, keepdims=True)
            for q in range(count)
        ],
        axis=0,
    )


def setup_kernel(devices, cap_rows, owner, column, coef, weight, counts, out, acc, offset):
    acc[...] = jnp.zeros_like(acc)
    offset[...] = jnp.zeros_like(offset)
    later = (
        lax.broadcasted_iota(jnp.int32, (BLOCK_SLOTS, BLOCK_SLOTS), 0)
        <= lax.broadcasted_iota(jnp.int32, (BLOCK_SLOTS, BLOCK_SLOTS), 1)
    )
    later = jnp.where(later, 1.0, 0.0).astype(jnp.bfloat16)
    within = lax.broadcasted_iota(jnp.int32, (1, BLOCK_SLOTS), 1)

    def block(i, _):
        own = pair(owner, i)
        named = jnp.where(onehot(own, devices), 1.0, 0.0)
        running = (
            jnp.dot(named.astype(jnp.bfloat16), later, preferred_element_type=jnp.float32)
            + offset[:, 0:1]
        )
        rank = (jnp.sum(named * running, axis=0, keepdims=True) - 1.0).astype(jnp.int32)
        offset[...] += jnp.broadcast_to(jnp.sum(named, axis=1, keepdims=True), offset.shape)
        live = within < counts[pl.ds(i, 1), 0:1]
        gain = jnp.where(live, pair(coef, i), 0.0)
        flow = pair(weight, i) * gain
        gain_high, gain_low = split(gain)
        flow_high, flow_low = split(flow)
        values = jnp.concatenate(
            [
                jnp.full((1, BLOCK_SLOTS), i, jnp.int32).astype(jnp.float32),
                pair(column, i).astype(jnp.float32),
                gain_high,
                gain_low,
                flow_high,
                flow_low,
            ],
            axis=0,
        )
        acc[...] += lax.dot_general(
            spread(one_hot(own * cap_rows + rank // LANES, LANES), values),
            lanes_map(rank % LANES),
            (((1,), (1,)), ((), ())),
            preferred_element_type=jnp.float32,
        )
        return 0

    lax.fori_loop(0, owner.shape[0] // 2, block, 0, unroll=4)
    out[0] = acc[0:128]
    out[1] = acc[128:256]
    out[2] = acc[256:384] + acc[384:512]
    out[3] = acc[512:640] + acc[640:768]


def setup(owner, column, coef, weight, counts, devices, cap_rows):
    return pl.pallas_call(
        functools.partial(setup_kernel, devices, cap_rows),
        out_shape=jax.ShapeDtypeStruct((4, LANES, LANES), jnp.float32),
        scratch_shapes=[
            pltpu.VMEM((6 * LANES, LANES), jnp.float32),
            pltpu.VMEM((devices, LANES), jnp.float32),
        ],
        compiler_params=PARAMS,
    )(owner, column, coef, weight, counts)


def level_down(mix, air, k, under, carried):
    coupling = mix[k : k + 1, :]
    inverse = 1.0 / (1.0 + coupling + under)
    part = (air[k] + carried) * inverse
    ratio = coupling * inverse
    return part, ratio, inverse, ratio * (1.0 + under), coupling * part


def descend_end_kernel(air, mix, end):
    under = jnp.zeros((1, end.shape[1]), jnp.float32)
    carried = jnp.zeros((air.shape[0], end.shape[1]), jnp.float32)
    levels_first = jnp.swapaxes(air[...], 0, 1)
    for k in range(air.shape[1]):
        _, _, _, under, carried = level_down(mix, levels_first, k, under, carried)
    end[...] = jnp.concatenate([carried, under], axis=0)


def descend_end(air, mix):
    tracers, levels, columns = air.shape
    return pl.pallas_call(
        descend_end_kernel,
        grid=(columns // COL_TILE,),
        in_specs=[
            pl.BlockSpec((tracers, levels, COL_TILE), lambda j: (0, 0, j)),
            pl.BlockSpec((levels, COL_TILE), lambda j: (0, j)),
        ],
        out_specs=pl.BlockSpec((tracers + 1, COL_TILE), lambda j: (0, j)),
        out_shape=jax.ShapeDtypeStruct((tracers + 1, columns), jnp.float32),
        compiler_params=PARAMS,
    )(air, mix)


def descend_kernel(air, mix, start, last, parts, ratios, ends):
    tracers, levels, _ = air.shape
    levels_first = jnp.swapaxes(air[...], 0, 1)
    carried = start[0:tracers, :]
    under = start[tracers : tracers + 1, :]
    for k in range(levels):
        part, ratio, inverse, under, carried = level_down(mix, levels_first, k, under, carried)
        parts[k] = part
        if k == levels - 1:
            ratio = last[...] * inverse
        ratios[k : k + 1, :] = ratio
    value, factor = part, ratio
    ends[0, 0:tracers, :] = part
    ends[0, tracers : tracers + 1, :] = ratio
    for k in range(levels - 2, -1, -1):
        ratio = ratios[k : k + 1, :]
        value = parts[k] + ratio * value
        factor = ratio * factor
    ends[1, 0:tracers, :] = value
    ends[1, tracers : tracers + 1, :] = factor


def descend(air, mix, start, last):
    tracers, levels, columns = air.shape
    return pl.pallas_call(
        descend_kernel,
        grid=(columns // COL_TILE,),
        in_specs=[
            pl.BlockSpec((tracers, levels, COL_TILE), lambda j: (0, 0, j)),
            pl.BlockSpec((levels, COL_TILE), lambda j: (0, j)),
            pl.BlockSpec((tracers + 1, COL_TILE), lambda j: (0, j)),
            pl.BlockSpec((1, COL_TILE), lambda j: (0, j)),
        ],
        out_specs=[
            pl.BlockSpec((levels, tracers, COL_TILE), lambda j: (0, 0, j)),
            pl.BlockSpec((levels, COL_TILE), lambda j: (0, j)),
            pl.BlockSpec((2, tracers + 1, COL_TILE), lambda j: (0, 0, j)),
        ],
        out_shape=[
            jax.ShapeDtypeStruct((levels, tracers, columns), jnp.float32),
            jax.ShapeDtypeStruct(mix.shape, jnp.float32),
            jax.ShapeDtypeStruct((2, tracers + 1, columns), jnp.float32),
        ],
        compiler_params=PARAMS,
    )(air, mix, start, last)


def ascend_kernel(parts, ratios, below, out):
    value = below[...]
    risen = []
    for k in range(parts.shape[0] - 1, -1, -1):
        value = parts[k] + ratios[k : k + 1, :] * value
        risen.append(value)
    out[...] = jnp.swapaxes(jnp.stack(risen[::-1]), 0, 1)


def ascend(parts, ratios, below):
    levels, tracers, columns = parts.shape
    return pl.pallas_call(
        ascend_kernel,
        grid=(columns // COL_TILE,),
        in_specs=[
            pl.BlockSpec((levels, tracers, COL_TILE), lambda j: (0, 0, j)),
            pl.BlockSpec((levels, COL_TILE), lambda j: (0, j)),
            pl.BlockSpec((tracers, COL_TILE), lambda j: (0, j)),
        ],
        out_specs=pl.BlockSpec((tracers, levels, COL_TILE), lambda j: (0, 0, j)),
        out_shape=jax.ShapeDtypeStruct((tracers, levels, columns), jnp.float32),
        compiler_params=PARAMS,
    )(parts, ratios, below)


def exchange_kernel(
    tracers,
    sections,
    ring,
    resid,
    slope,
    flux,
    other,
    block,
    column,
    flow,
    gain,
    frac,
    row,
    lane,
    sea,
    rate,
    flux_new,
    sea_new,
    sent,
    arrived,
    back,
    returned,
    acc,
    out_send,
    out_recv,
    back_send,
    back_recv,
):
    devices = sections * ring
    rows, surf_rows = slope.shape[0], rate.shape[0]
    parts = back.shape[1] // tracers
    acc_rows = acc.shape[0] // (tracers + 1)
    me = lax.axis_index("sect") * ring + lax.axis_index("cols")

    def coords(device):
        return (device // ring, lax.rem(device, ring))

    def ahead(s):
        return lax.rem(me + s, devices)

    def behind(s):
        return lax.rem(me + devices - s, devices)

    def outward(s):
        device = ahead(s)
        return pltpu.make_async_remote_copy(
            src_ref=sent.at[device],
            dst_ref=arrived.at[me],
            send_sem=out_send.at[s],
            recv_sem=out_recv.at[s],
            device_id=coords(device),
            device_id_type=pl.DeviceIdType.MESH,
        )

    def homeward(s):
        device = ahead(s)
        return pltpu.make_async_remote_copy(
            src_ref=back.at[device],
            dst_ref=returned.at[me],
            send_sem=back_send.at[s],
            recv_sem=back_recv.at[s],
            device_id=coords(device),
            device_id_type=pl.DeviceIdType.MESH,
        )

    def pack(values):
        return jnp.concatenate(
            [values[:, p * LANES : (p + 1) * LANES] for p in range(parts)], axis=0
        )

    def unpack(values):
        count = values.shape[0] // parts
        return jnp.concatenate([values[p * count : (p + 1) * count] for p in range(parts)], axis=1)

    barrier = pltpu.get_barrier_semaphore()

    def greet(s, _):
        pl.semaphore_signal(
            barrier,
            inc=1,
            device_id=coords(ahead(s)),
            device_id_type=pl.DeviceIdType.MESH,
        )
        return 0

    lax.fori_loop(1, devices, greet, 0)
    bottom = resid[...] + jnp.concatenate([slope[...]] * tracers, axis=0) * (flux[...] + other[...])
    table = table_of(bottom)

    def at_cells(device):
        here = pl.ds(device, 1)
        picked = gather_step(table, block[here, :], column[here, :], rows, tracers)
        return pack(jnp.concatenate([picked, gain[here, :]], axis=0))

    own = at_cells(me)
    sent[me] = own
    pl.semaphore_wait(barrier, devices - 1)

    def send(s, _):
        device = ahead(s)
        sent[device] = at_cells(device)
        outward(s).start()
        return 0

    lax.fori_loop(1, devices, send, 0)
    acc[...] = jnp.zeros_like(acc)

    def add(values, device):
        here = pl.ds(device, 1)
        came = unpack(values)
        strength = came[tracers:] * frac[here, :]
        scatter_step(
            acc,
            jnp.concatenate([came[0:tracers] * strength, strength], axis=0),
            row[here, :],
            lane[here, :],
            acc_rows,
        )

    add(own, me)

    def receive(s, _):
        outward(s).wait_recv()
        device = behind(s)
        add(arrived[device], device)
        return 0

    lax.fori_loop(1, devices, receive, 0)
    pace = rate[...]
    inverse = 1.0 / (1.0 + pace * acc[tracers * acc_rows : tracers * acc_rows + surf_rows])
    for q in range(tracers):
        here = slice(q * surf_rows, (q + 1) * surf_rows)
        summed = acc[q * acc_rows : q * acc_rows + surf_rows]
        sea_new[here] = (sea[here] + pace * summed) * inverse
    sea_table = table_of(sea_new[...])

    def seen(device):
        here = pl.ds(device, 1)
        return pack(gather_step(sea_table, row[here, :], lane[here, :], surf_rows, tracers))

    def give_back(s, _):
        device = ahead(s)
        back[device] = seen(device)
        homeward(s).start()
        return 0

    lax.fori_loop(1, devices, give_back, 0)
    flux_new[...] = jnp.zeros_like(flux_new)

    def collect(values, device):
        here = pl.ds(device, 1)
        scatter_step(
            flux_new,
            (unpack(values) - unpack(sent[device])[0:tracers]) * flow[here, :],
            block[here, :],
            column[here, :],
            rows,
        )

    collect(seen(me), me)

    def take_back(s, _):
        homeward(s).wait_recv()
        device = behind(s)
        collect(returned[device], device)
        return 0

    lax.fori_loop(1, devices, take_back, 0)

    def finish(s, _):
        outward(s).wait_send()
        homeward(s).wait_send()
        return 0

    lax.fori_loop(1, devices, finish, 0)


def exchange(tracers, sections, ring, resid, slope, flux, other, block, column, flow, *surface):
    devices, slots = block.shape
    surf_rows = surface[-1].shape[0]
    outgoing = pltpu.VMEM((devices, (tracers + 1) * slots // LANES, LANES), jnp.float32)
    homecoming = pltpu.VMEM((devices, tracers * slots // LANES, LANES), jnp.float32)
    return pl.pallas_call(
        functools.partial(exchange_kernel, tracers, sections, ring),
        out_shape=[
            jax.ShapeDtypeStruct(resid.shape, jnp.float32),
            jax.ShapeDtypeStruct((tracers * surf_rows, LANES), jnp.float32),
        ],
        in_specs=[pl.BlockSpec(memory_space=pltpu.VMEM)] * 13,
        out_specs=[pl.BlockSpec(memory_space=pltpu.VMEM)] * 2,
        scratch_shapes=[
            outgoing,
            outgoing,
            homecoming,
            homecoming,
            pltpu.VMEM(((tracers + 1) * (-(-surf_rows // 16) * 16), LANES), jnp.float32),
            pltpu.SemaphoreType.DMA((devices,)),
            pltpu.SemaphoreType.DMA((devices,)),
            pltpu.SemaphoreType.DMA((devices,)),
            pltpu.SemaphoreType.DMA((devices,)),
        ],
        compiler_params=pltpu.CompilerParams(
            vmem_limit_bytes=40 * 1024 * 1024, collective_id=0, has_side_effects=True
        ),
    )(resid, slope, flux, other, block, column, flow, *surface)


def body(
    air_state,
    mix_coef,
    flux_scale,
    sea_state,
    sea_rate,
    block_counts,
    cell_column,
    cell_owner,
    cell_coef,
    cell_weight,
    slot_cell,
    slot_frac,
):
    levels, tracers, columns = air_state.shape
    is_lower = lax.axis_index("sect") == 1
    devices = lax.axis_size("sect") * lax.axis_size("cols")
    rows = columns // BLOCK_COLS
    surf_cells = sea_state.shape[1]
    surf_rows = surf_cells // LANES
    capacity = slot_cell.shape[0] // devices
    cap_rows = -(-capacity // LANES)
    padding = ((0, 0), (0, cap_rows * LANES - capacity))

    air = jnp.swapaxes(air_state, 0, 1)
    handed = lax.ppermute(descend_end(air, mix_coef), "sect", [(0, 1)])
    slots = setup(
        cell_owner.reshape(-1, LANES),
        cell_column.reshape(-1, LANES),
        cell_coef.reshape(-1, LANES),
        cell_weight.reshape(-1, LANES),
        jnp.broadcast_to(block_counts.reshape(-1, 1), (rows, LANES)),
        devices,
        cap_rows,
    )
    slots = slots.reshape(4, LANES * LANES)[:, : devices * cap_rows * LANES]
    slots = slots.reshape(4, devices, cap_rows * LANES)
    block = slots[0].astype(jnp.int32)
    column = slots[1].astype(jnp.int32)
    cell = jnp.pad(slot_cell.reshape(devices, capacity), padding)
    frac = jnp.pad(slot_frac.reshape(devices, capacity), padding)
    row, lane = cell // LANES, cell % LANES

    last = jnp.where(is_lower, flux_scale, mix_coef[-1])[None]
    parts, ratios, ends = descend(air, mix_coef, handed, last)
    received = lax.ppermute(ends, "sect", [(1, 0)])
    low = jnp.where(is_lower, ends, received)
    resid = low[0, :tracers].reshape(tracers * rows, LANES)
    slope = low[0, tracers].reshape(rows, LANES)

    sea = sea_state.reshape(tracers * surf_rows, LANES)
    rate = sea_rate.reshape(surf_rows, LANES)
    flux = other = jnp.zeros((tracers * rows, LANES), jnp.float32)
    for _ in range(SUBSTEPS):
        flux, sea = exchange(
            tracers,
            lax.axis_size("sect"),
            lax.axis_size("cols"),
            resid,
            slope,
            flux,
            other,
            block,
            column,
            slots[3],
            slots[2],
            frac,
            row,
            lane,
            sea,
            rate,
        )
        other = lax.ppermute(flux, "sect", [(0, 1), (1, 0)])
    flux_col = (flux + other).reshape(tracers, columns)
    below = jnp.where(is_lower, flux_col, low[1, :tracers] + low[1, tracers] * flux_col)
    return (jnp.swapaxes(ascend(parts, ratios, below), 0, 1), sea.reshape(tracers, surf_cells))


def solution(mesh):
    return jax.shard_map(
        body,
        mesh=mesh,
        in_specs=(
            P("sect", None, "cols"),
            P("sect", "cols"),
            P("cols"),
            P(None, ("sect", "cols")),
            P(("sect", "cols")),
            P(("sect", "cols"), None),
            P(("sect", "cols")),
            P(("sect", "cols"), None),
            P(("sect", "cols")),
            P(("sect", "cols")),
            P(("sect", "cols")),
            P(("sect", "cols")),
        ),
        out_specs=(P("sect", None, "cols"), P(None, ("sect", "cols"))),
        check_vma=False,
    )
```

```python
import functools

import jax
import jax.numpy as jnp
from jax import lax
from jax.experimental import pallas as pl
from jax.experimental.pallas import tpu as pltpu
from jax.sharding import PartitionSpec as P

BLOCK_COLS = 128
BLOCK_SLOTS = 256
SUBSTEPS = 2
LANES = 128
COL_TILE = 1024
PARAMS = pltpu.CompilerParams(vmem_limit_bytes=40 * 1024 * 1024)


def split(value):
    high = value.astype(jnp.bfloat16).astype(jnp.float32)
    return high, value - high


def pair(ref, i):
    return jnp.concatenate([ref[pl.ds(2 * i, 1), :], ref[pl.ds(2 * i + 1, 1), :]], axis=1)


def onehot(index, count):
    return lax.broadcasted_iota(jnp.int32, (count, index.shape[1]), 0) == index


def lanes_map(lane):
    return jnp.where(onehot(lane, LANES), 1.0, 0.0).astype(jnp.bfloat16)


def spread(mask, values):
    values = values.astype(jnp.bfloat16)
    return jnp.concatenate([mask * values[q : q + 1] for q in range(values.shape[0])], axis=0)


def one_hot(index, count):
    return jnp.where(onehot(index, count), 1.0, 0.0).astype(jnp.bfloat16)


def scatter_step(acc, values, row, lane, rows):
    mask = one_hot(row, rows)
    high, low = split(values)
    lane_hot = lanes_map(lane)
    acc[...] += lax.dot_general(
        jnp.concatenate([spread(mask, high), spread(mask, low)], axis=1),
        jnp.concatenate([lane_hot, lane_hot], axis=1),
        (((1,), (1,)), ((), ())),
        preferred_element_type=jnp.float32,
    )


def table_of(value):
    high, low = split(value)
    return jnp.concatenate([high, low], axis=1).astype(jnp.bfloat16)


def gather_step(table, row, lane, rows, count):
    lane_hot = lanes_map(lane)
    picked = jnp.dot(
        table, jnp.concatenate([lane_hot, lane_hot], axis=0), preferred_element_type=jnp.float32
    )
    mask = onehot(row, rows)
    return jnp.concatenate(
        [
            jnp.sum(jnp.where(mask, picked[q * rows : (q + 1) * rows], 0.0), axis=0, keepdims=True)
            for q in range(count)
        ],
        axis=0,
    )


def setup_kernel(devices, cap_rows, owner, column, coef, weight, counts, out, acc, offset):
    acc[...] = jnp.zeros_like(acc)
    offset[...] = jnp.zeros_like(offset)
    later = (
        lax.broadcasted_iota(jnp.int32, (BLOCK_SLOTS, BLOCK_SLOTS), 0)
        <= lax.broadcasted_iota(jnp.int32, (BLOCK_SLOTS, BLOCK_SLOTS), 1)
    )
    later = jnp.where(later, 1.0, 0.0).astype(jnp.bfloat16)
    within = lax.broadcasted_iota(jnp.int32, (1, BLOCK_SLOTS), 1)

    def block(i, _):
        own = pair(owner, i)
        named = jnp.where(onehot(own, devices), 1.0, 0.0)
        running = (
            jnp.dot(named.astype(jnp.bfloat16), later, preferred_element_type=jnp.float32)
            + offset[:, 0:1]
        )
        rank = (jnp.sum(named * running, axis=0, keepdims=True) - 1.0).astype(jnp.int32)
        offset[...] += jnp.broadcast_to(jnp.sum(named, axis=1, keepdims=True), offset.shape)
        live = within < counts[pl.ds(i, 1), 0:1]
        gain = jnp.where(live, pair(coef, i), 0.0)
        flow = pair(weight, i) * gain
        gain_high, gain_low = split(gain)
        flow_high, flow_low = split(flow)
        values = jnp.concatenate(
            [
                jnp.full((1, BLOCK_SLOTS), i, jnp.int32).astype(jnp.float32),
                pair(column, i).astype(jnp.float32),
                gain_high,
                gain_low,
                flow_high,
                flow_low,
            ],
            axis=0,
        )
        acc[...] += lax.dot_general(
            spread(one_hot(own * cap_rows + rank // LANES, LANES), values),
            lanes_map(rank % LANES),
            (((1,), (1,)), ((), ())),
            preferred_element_type=jnp.float32,
        )
        return 0

    lax.fori_loop(0, owner.shape[0] // 2, block, 0, unroll=4)
    out[0] = acc[0:128]
    out[1] = acc[128:256]
    out[2] = acc[256:384] + acc[384:512]
    out[3] = acc[512:640] + acc[640:768]


def setup(owner, column, coef, weight, counts, devices, cap_rows):
    return pl.pallas_call(
        functools.partial(setup_kernel, devices, cap_rows),
        out_shape=jax.ShapeDtypeStruct((4, LANES, LANES), jnp.float32),
        scratch_shapes=[
            pltpu.VMEM((6 * LANES, LANES), jnp.float32),
            pltpu.VMEM((devices, LANES), jnp.float32),
        ],
        compiler_params=PARAMS,
    )(owner, column, coef, weight, counts)


def level_down(mix, air, k, under, carried):
    coupling = mix[k : k + 1, :]
    inverse = 1.0 / (1.0 + coupling + under)
    part = (air[k] + carried) * inverse
    ratio = coupling * inverse
    return part, ratio, inverse, ratio * (1.0 + under), coupling * part


def descend_end_kernel(air, mix, end):
    under = jnp.zeros((1, end.shape[1]), jnp.float32)
    carried = jnp.zeros((air.shape[0], end.shape[1]), jnp.float32)
    levels_first = jnp.swapaxes(air[...], 0, 1)
    for k in range(air.shape[1]):
        _, _, _, under, carried = level_down(mix, levels_first, k, under, carried)
    end[...] = jnp.concatenate([carried, under], axis=0)


def descend_end(air, mix):
    tracers, levels, columns = air.shape
    return pl.pallas_call(
        descend_end_kernel,
        grid=(columns // COL_TILE,),
        in_specs=[
            pl.BlockSpec((tracers, levels, COL_TILE), lambda j: (0, 0, j)),
            pl.BlockSpec((levels, COL_TILE), lambda j: (0, j)),
        ],
        out_specs=pl.BlockSpec((tracers + 1, COL_TILE), lambda j: (0, j)),
        out_shape=jax.ShapeDtypeStruct((tracers + 1, columns), jnp.float32),
        compiler_params=PARAMS,
    )(air, mix)


def descend_kernel(air, mix, start, last, parts, ratios, ends):
    tracers, levels, _ = air.shape
    levels_first = jnp.swapaxes(air[...], 0, 1)
    carried = start[0:tracers, :]
    under = start[tracers : tracers + 1, :]
    for k in range(levels):
        part, ratio, inverse, under, carried = level_down(mix, levels_first, k, under, carried)
        parts[k] = part
        if k == levels - 1:
            ratio = last[...] * inverse
        ratios[k : k + 1, :] = ratio
    value, factor = part, ratio
    ends[0, 0:tracers, :] = part
    ends[0, tracers : tracers + 1, :] = ratio
    for k in range(levels - 2, -1, -1):
        ratio = ratios[k : k + 1, :]
        value = parts[k] + ratio * value
        factor = ratio * factor
    ends[1, 0:tracers, :] = value
    ends[1, tracers : tracers + 1, :] = factor


def descend(air, mix, start, last):
    tracers, levels, columns = air.shape
    return pl.pallas_call(
        descend_kernel,
        grid=(columns // COL_TILE,),
        in_specs=[
            pl.BlockSpec((tracers, levels, COL_TILE), lambda j: (0, 0, j)),
            pl.BlockSpec((levels, COL_TILE), lambda j: (0, j)),
            pl.BlockSpec((tracers + 1, COL_TILE), lambda j: (0, j)),
            pl.BlockSpec((1, COL_TILE), lambda j: (0, j)),
        ],
        out_specs=[
            pl.BlockSpec((levels, tracers, COL_TILE), lambda j: (0, 0, j)),
            pl.BlockSpec((levels, COL_TILE), lambda j: (0, j)),
            pl.BlockSpec((2, tracers + 1, COL_TILE), lambda j: (0, 0, j)),
        ],
        out_shape=[
            jax.ShapeDtypeStruct((levels, tracers, columns), jnp.float32),
            jax.ShapeDtypeStruct(mix.shape, jnp.float32),
            jax.ShapeDtypeStruct((2, tracers + 1, columns), jnp.float32),
        ],
        compiler_params=PARAMS,
    )(air, mix, start, last)


def ascend_kernel(parts, ratios, below, out):
    value = below[...]
    risen = []
    for k in range(parts.shape[0] - 1, -1, -1):
        value = parts[k] + ratios[k : k + 1, :] * value
        risen.append(value)
    out[...] = jnp.swapaxes(jnp.stack(risen[::-1]), 0, 1)


def ascend(parts, ratios, below):
    levels, tracers, columns = parts.shape
    return pl.pallas_call(
        ascend_kernel,
        grid=(columns // COL_TILE,),
        in_specs=[
            pl.BlockSpec((levels, tracers, COL_TILE), lambda j: (0, 0, j)),
            pl.BlockSpec((levels, COL_TILE), lambda j: (0, j)),
            pl.BlockSpec((tracers, COL_TILE), lambda j: (0, j)),
        ],
        out_specs=pl.BlockSpec((tracers, levels, COL_TILE), lambda j: (0, 0, j)),
        out_shape=jax.ShapeDtypeStruct((tracers, levels, columns), jnp.float32),
        compiler_params=PARAMS,
    )(parts, ratios, below)


def exchange_kernel(
    tracers,
    sections,
    ring,
    resid,
    slope,
    flux,
    other,
    block,
    column,
    flow,
    gain,
    frac,
    row,
    lane,
    sea,
    rate,
    flux_new,
    sea_new,
    sent,
    arrived,
    back,
    returned,
    acc,
    out_send,
    out_recv,
    back_send,
    back_recv,
):
    devices = sections * ring
    rows, surf_rows = slope.shape[0], rate.shape[0]
    parts = back.shape[1] // tracers
    acc_rows = acc.shape[0] // (tracers + 1)
    me = lax.axis_index("sect") * ring + lax.axis_index("cols")

    def coords(device):
        return (device // ring, lax.rem(device, ring))

    def ahead(s):
        return lax.rem(me + s, devices)

    def behind(s):
        return lax.rem(me + devices - s, devices)

    def outward(s):
        device = ahead(s)
        return pltpu.make_async_remote_copy(
            src_ref=sent.at[device],
            dst_ref=arrived.at[me],
            send_sem=out_send.at[s],
            recv_sem=out_recv.at[s],
            device_id=coords(device),
            device_id_type=pl.DeviceIdType.MESH,
        )

    def homeward(s):
        device = ahead(s)
        return pltpu.make_async_remote_copy(
            src_ref=back.at[device],
            dst_ref=returned.at[me],
            send_sem=back_send.at[s],
            recv_sem=back_recv.at[s],
            device_id=coords(device),
            device_id_type=pl.DeviceIdType.MESH,
        )

    def pack(values):
        return jnp.concatenate(
            [values[:, p * LANES : (p + 1) * LANES] for p in range(parts)], axis=0
        )

    def unpack(values):
        count = values.shape[0] // parts
        return jnp.concatenate([values[p * count : (p + 1) * count] for p in range(parts)], axis=1)

    def rows_of(ref, sources):
        return jnp.concatenate([ref[pl.ds(source, 1), :] for source in sources], axis=1)

    def in_pairs(act):
        act(1)

        def both(p, _):
            act(2 * p, 2 * p + 1)
            return 0

        lax.fori_loop(1, devices // 2, both, 0)

    barrier = pltpu.get_barrier_semaphore()

    def greet(s, _):
        pl.semaphore_signal(
            barrier,
            inc=1,
            device_id=coords(ahead(s)),
            device_id_type=pl.DeviceIdType.MESH,
        )
        return 0

    lax.fori_loop(1, devices, greet, 0)
    bottom = resid[...] + jnp.concatenate([slope[...]] * tracers, axis=0) * (flux[...] + other[...])
    table = table_of(bottom)

    def at_cells(device):
        here = pl.ds(device, 1)
        picked = gather_step(table, block[here, :], column[here, :], rows, tracers)
        return pack(jnp.concatenate([picked, gain[here, :]], axis=0))

    own = at_cells(me)
    sent[me] = own
    pl.semaphore_wait(barrier, devices - 1)

    def send(*steps):
        chunks = [at_cells(ahead(s)) for s in steps]
        for s, chunk in zip(steps, chunks):
            sent[ahead(s)] = chunk
        for s in steps:
            outward(s).start()

    in_pairs(send)
    acc[...] = jnp.zeros_like(acc)

    def add(chunks, sources):
        came = jnp.concatenate([unpack(chunk) for chunk in chunks], axis=1)
        strength = came[tracers:] * rows_of(frac, sources)
        scatter_step(
            acc,
            jnp.concatenate([came[0:tracers] * strength, strength], axis=0),
            rows_of(row, sources),
            rows_of(lane, sources),
            acc_rows,
        )

    add([own], [me])

    def receive(*steps):
        for s in steps:
            outward(s).wait_recv()
        add([arrived[behind(s)] for s in steps], [behind(s) for s in steps])

    in_pairs(receive)
    pace = rate[...]
    inverse = 1.0 / (1.0 + pace * acc[tracers * acc_rows : tracers * acc_rows + surf_rows])
    for q in range(tracers):
        here = slice(q * surf_rows, (q + 1) * surf_rows)
        summed = acc[q * acc_rows : q * acc_rows + surf_rows]
        sea_new[here] = (sea[here] + pace * summed) * inverse
    sea_table = table_of(sea_new[...])

    def seen(device):
        here = pl.ds(device, 1)
        return pack(gather_step(sea_table, row[here, :], lane[here, :], surf_rows, tracers))

    def give_back(*steps):
        chunks = [seen(ahead(s)) for s in steps]
        for s, chunk in zip(steps, chunks):
            back[ahead(s)] = chunk
        for s in steps:
            homeward(s).start()

    in_pairs(give_back)
    flux_new[...] = jnp.zeros_like(flux_new)

    def collect(chunks, sources):
        change = [
            unpack(chunk) - unpack(sent[source])[0:tracers]
            for chunk, source in zip(chunks, sources)
        ]
        scatter_step(
            flux_new,
            jnp.concatenate(change, axis=1) * rows_of(flow, sources),
            rows_of(block, sources),
            rows_of(column, sources),
            rows,
        )

    collect([seen(me)], [me])

    def take_back(*steps):
        for s in steps:
            homeward(s).wait_recv()
        collect([returned[behind(s)] for s in steps], [behind(s) for s in steps])

    in_pairs(take_back)

    def finish(s, _):
        outward(s).wait_send()
        homeward(s).wait_send()
        return 0

    lax.fori_loop(1, devices, finish, 0)


def exchange(tracers, sections, ring, resid, slope, flux, other, block, column, flow, *surface):
    devices, slots = block.shape
    surf_rows = surface[-1].shape[0]
    outgoing = pltpu.VMEM((devices, (tracers + 1) * slots // LANES, LANES), jnp.float32)
    homecoming = pltpu.VMEM((devices, tracers * slots // LANES, LANES), jnp.float32)
    return pl.pallas_call(
        functools.partial(exchange_kernel, tracers, sections, ring),
        out_shape=[
            jax.ShapeDtypeStruct(resid.shape, jnp.float32),
            jax.ShapeDtypeStruct((tracers * surf_rows, LANES), jnp.float32),
        ],
        in_specs=[pl.BlockSpec(memory_space=pltpu.VMEM)] * 13,
        out_specs=[pl.BlockSpec(memory_space=pltpu.VMEM)] * 2,
        scratch_shapes=[
            outgoing,
            outgoing,
            homecoming,
            homecoming,
            pltpu.VMEM(((tracers + 1) * (-(-surf_rows // 16) * 16), LANES), jnp.float32),
            pltpu.SemaphoreType.DMA((devices,)),
            pltpu.SemaphoreType.DMA((devices,)),
            pltpu.SemaphoreType.DMA((devices,)),
            pltpu.SemaphoreType.DMA((devices,)),
        ],
        compiler_params=pltpu.CompilerParams(
            vmem_limit_bytes=40 * 1024 * 1024, collective_id=0, has_side_effects=True
        ),
    )(resid, slope, flux, other, block, column, flow, *surface)


def body(
    air_state,
    mix_coef,
    flux_scale,
    sea_state,
    sea_rate,
    block_counts,
    cell_column,
    cell_owner,
    cell_coef,
    cell_weight,
    slot_cell,
    slot_frac,
):
    levels, tracers, columns = air_state.shape
    is_lower = lax.axis_index("sect") == 1
    devices = lax.axis_size("sect") * lax.axis_size("cols")
    rows = columns // BLOCK_COLS
    surf_cells = sea_state.shape[1]
    surf_rows = surf_cells // LANES
    capacity = slot_cell.shape[0] // devices
    cap_rows = -(-capacity // LANES)
    padding = ((0, 0), (0, cap_rows * LANES - capacity))

    air = jnp.swapaxes(air_state, 0, 1)
    handed = lax.ppermute(descend_end(air, mix_coef), "sect", [(0, 1)])
    slots = setup(
        cell_owner.reshape(-1, LANES),
        cell_column.reshape(-1, LANES),
        cell_coef.reshape(-1, LANES),
        cell_weight.reshape(-1, LANES),
        jnp.broadcast_to(block_counts.reshape(-1, 1), (rows, LANES)),
        devices,
        cap_rows,
    )
    slots = slots.reshape(4, LANES * LANES)[:, : devices * cap_rows * LANES]
    slots = slots.reshape(4, devices, cap_rows * LANES)
    block = slots[0].astype(jnp.int32)
    column = slots[1].astype(jnp.int32)
    cell = jnp.pad(slot_cell.reshape(devices, capacity), padding)
    frac = jnp.pad(slot_frac.reshape(devices, capacity), padding)
    row, lane = cell // LANES, cell % LANES

    last = jnp.where(is_lower, flux_scale, mix_coef[-1])[None]
    parts, ratios, ends = descend(air, mix_coef, handed, last)
    received = lax.ppermute(ends, "sect", [(1, 0)])
    low = jnp.where(is_lower, ends, received)
    resid = low[0, :tracers].reshape(tracers * rows, LANES)
    slope = low[0, tracers].reshape(rows, LANES)

    sea = sea_state.reshape(tracers * surf_rows, LANES)
    rate = sea_rate.reshape(surf_rows, LANES)
    flux = other = jnp.zeros((tracers * rows, LANES), jnp.float32)
    for _ in range(SUBSTEPS):
        flux, sea = exchange(
            tracers,
            lax.axis_size("sect"),
            lax.axis_size("cols"),
            resid,
            slope,
            flux,
            other,
            block,
            column,
            slots[3],
            slots[2],
            frac,
            row,
            lane,
            sea,
            rate,
        )
        other = lax.ppermute(flux, "sect", [(0, 1), (1, 0)])
    flux_col = (flux + other).reshape(tracers, columns)
    below = jnp.where(is_lower, flux_col, low[1, :tracers] + low[1, tracers] * flux_col)
    return (jnp.swapaxes(ascend(parts, ratios, below), 0, 1), sea.reshape(tracers, surf_cells))


def solution(mesh):
    return jax.shard_map(
        body,
        mesh=mesh,
        in_specs=(
            P("sect", None, "cols"),
            P("sect", "cols"),
            P("cols"),
            P(None, ("sect", "cols")),
            P(("sect", "cols")),
            P(("sect", "cols"), None),
            P(("sect", "cols")),
            P(("sect", "cols"), None),
            P(("sect", "cols")),
            P(("sect", "cols")),
            P(("sect", "cols")),
            P(("sect", "cols")),
        ),
        out_specs=(P("sect", None, "cols"), P(None, ("sect", "cols"))),
        check_vma=False,
    )
```
